32 devices in a mesh: groups: 2 (over y), loop: 4 (over z), hid: 4 (over x, core).
Axes of the slice: x: 2, y: 2, z: 4, core: 2. Of those that a mesh axis runs over, the one named last changes fastest.
Arguments:
- tokens: bfloat16 [2048, 2048], P(('groups', 'loop')), parts along dimension 0, may hold values from -6 to 6
- route_ids: int32 [2048, 8], P(('groups', 'loop')), parts along dimension 0, may hold values from 0 to 127, all different within a row; in each aligned block of 256 rows (0 to 255, 256 to 511, ...) at most 32 rows name the same one
- router_weights: float32 [2048, 8], P(('groups', 'loop')), parts along dimension 0, may hold values from 1 to 3
- accepted: int32 [2048], P(('groups', 'loop')), parts along dimension 0, may hold values 0 or 1
- parents: int32 [2048], P(('groups', 'loop')), parts along dimension 0, may hold values from 0 to 62, as said below
- expert_weights: bfloat16 [4, 3, 1536, 2048], P(None, None, 'hid', 'loop'), may hold values from -0.125 to 0.125
Outputs:
- expert_out: bfloat16 [2048, 2048], P(('groups', 'loop'), 'hid'), parts along dimension 0
- parent_out: bfloat16 [2048, 2048], P(('groups', 'loop'), 'hid'), parts along dimension 0
The draws below stay inside these ranges and needn't reach their ends.
There are 2 independent parts, one for each index of `groups`. The reference program is written for one: setup_inputs(seed, part) draws one part's arguments, and reference() takes and returns one part's arrays. A program takes and returns all parts, laid end to end along the dimension named above; an argument that names none is the same for every part. Nothing has to cross between parts.
Inputs may be any that keep to these rules, and one draw needn't show every extreme that they name: `route_ids`: the 8 ids of a row are different; no expert is named by more than 32 of the rows of one index of loop, a bound that some block reaches. `parents`: A node's parent is an earlier node of the same tree; the first node of a tree is its own parent, and the last node's parent is the node just before it.
All inputs are finite; a program needn't handle non-finite values. No bound on the sum of `accepted` on one device may be relied on, other than what follows from the above.
Results may differ from the reference program's by a relative error of at most 0.005.
Values may be sent and summed in bfloat16 or wider, within the bound.
A program may use at most 64 MiB of HBM per device.

```python
import math
import jax
import jax.numpy as jnp
import numpy as np
from jax import lax

D = 2048
FF = 1536
LAYER_EXP = 128
E_WIN = 4
TOP = 8
NODES = 64
ROWS_DEV = 256
CAP = 32
ROWS = 1024


def draw_parents(key, part):
    key = jax.random.fold_in(key, 7)
    node_pos = jnp.arange(ROWS, dtype=jnp.int32) % NODES
    drawn = jax.random.randint(key, (ROWS,), 0, jnp.maximum(node_pos, 1), dtype=jnp.int32)
    return jnp.where(node_pos == NODES - 1, NODES - 2, drawn).astype(jnp.int32)


def plant(values, rng, smallest, high):
    spot = [jax.random.randint(jax.random.fold_in(rng, axis), (), 0, length) for axis, length in enumerate(values.shape)]
    longest = values.shape.index(max(values.shape))
    neighbour = spot[:longest] + [(spot[longest] + 1) % values.shape[longest]] + spot[longest + 1:]
    return values.at[tuple(spot)].set(smallest).at[tuple(neighbour)].set(high)


def level_of(own_key, dims, pieces, smallest, largest):
    factor_of, own = 1.0, jax.random.fold_in(own_key, 6)
    for position, shards_of in pieces:
        draws = jnp.exp(jax.random.uniform(jax.random.fold_in(own, position), (shards_of,), jnp.float32, smallest / len(pieces), largest / len(pieces)))
        factor_of = factor_of * jnp.repeat(draws, dims[position] // shards_of).reshape([-1 if axis == position else 1 for axis in range(len(dims))])
    return factor_of


def assign_block(own_key, own, number, rows, count, top, bound, slope):
    ranking = jax.random.permutation(own_key, count)
    crowded, ordinary = load_shares(count, rows * top, bound, slope, True), load_shares(count, rows * top, bound, slope, False)
    places = jnp.arange(count)

    def named(lengths, rotation):
        used = int((lengths > 0).sum())
        fixed = max(1, used // 4)
        moved = fixed + (places - fixed + rotation * (used - fixed)) % max(1, count - fixed)
        return jnp.zeros((count,), jnp.int32).at[ranking[jnp.where(places < fixed, places, moved)]].set(jnp.asarray(lengths, jnp.int32))

    lengths = jnp.where(number % 4 == 0, named(crowded, number // 4), named(ordinary, number - number // 4 - 1))
    mixed = jax.random.permutation(jax.random.fold_in(own, 3), count)
    giver, sink = mixed[0:count // 2 * 2:2], mixed[1:count // 2 * 2:2]
    margin = jnp.minimum(lengths[giver] - 1, bound - lengths[sink]) // 2
    margin = jnp.where((giver == ranking[0]) | (sink == ranking[0]) | (lengths[sink] == 0), 0, jnp.maximum(margin, 0))
    moved = jax.random.randint(jax.random.fold_in(own, 4), (count // 2,), 0, 1 << 20) % (margin + 1)
    lengths = lengths.at[giver].add(-moved).at[sink].add(moved)
    members = jnp.searchsorted(jnp.cumsum(lengths), jnp.arange(rows * top), side="right").astype(jnp.int32)
    listing = members.reshape(top, rows).T
    listing = listing[jax.random.permutation(jax.random.fold_in(own, 1), rows)]
    rotation = jax.random.randint(jax.random.fold_in(own, 2), (rows, 1), 0, top)
    return jnp.take_along_axis(listing, (jnp.arange(top)[None, :] + rotation) % top, axis=1)


def load_shares(count, total, most, slope, full):
    loads = [(1 << 20) // math.isqrt(grade ** slope) + 1 for grade in range(1, count + 1)]
    largest = most if full else min(most, max(-(-total // count), total * loads[0] // sum(loads)))
    least = 1 if total - largest >= count - 1 else 0
    given, surplus = [largest] + [least] * (count - 1), total - largest - least * (count - 1)
    while surplus > 0:
        candidates = [i for i in range(1, count) if given[i] < largest] or [i for i in range(1, count) if given[i] < most]
        mass, remaining = sum([loads[i] for i in candidates]), surplus
        for i in candidates:
            extra = min(most - given[i], max(1, remaining * loads[i] // mass), surplus)
            given[i] = given[i] + extra
            surplus = surplus - extra
    return np.array(given)


def gaussian(key, shape, deviation, limit, pieces=(), kind=jnp.bfloat16):
    array = deviation * jax.random.normal(key, shape, jnp.float32)
    if pieces:
        array = array * level_of(key, shape, pieces, -0.22, 0.18)
    return jnp.clip(array, -limit, limit).astype(kind)


def setup_inputs(seed: int = 0, part: int = 0) -> dict:
    arg_keys = jax.random.split(jax.random.key(seed), 7)
    part_keys = jax.random.split(jax.random.fold_in(arg_keys[6], part), 7)
    tokens = gaussian(part_keys[0], (ROWS, D), 1.0, 6.0, ((0, 4),))
    route_ids_keys = jax.random.split(jax.random.fold_in(part_keys[1], 1), ROWS // ROWS_DEV)
    route_ids_turns = jax.random.permutation(jax.random.fold_in(part_keys[1], 3), ROWS // ROWS_DEV)
    route_ids = jax.vmap(lambda own, number: assign_block(jax.random.fold_in(part_keys[1], 2), own, number, ROWS_DEV, LAYER_EXP, TOP, CAP, 2))(route_ids_keys, route_ids_turns).reshape((ROWS, TOP))
    router_weights = jnp.clip(1.0 + 2.0 * jax.random.uniform(part_keys[2], (ROWS, TOP), jnp.float32) ** level_of(part_keys[2], (ROWS, TOP), ((0, 4),), -0.2, 0.2), 1.0, 3.0)
    accepted = plant((jax.random.randint(part_keys[3], (ROWS,), 0, 8) < 7).astype(jnp.int32), jax.random.fold_in(part_keys[3], 1), 0, 1)
    parents = draw_parents(jax.random.fold_in(jax.random.fold_in(arg_keys[6], part), 71), part)
    expert_weights = gaussian(arg_keys[5], (E_WIN, 3, FF, D), D ** -0.5, 0.125, ((2, 4), (3, 4)))
    return {"tokens": tokens, "route_ids": route_ids, "router_weights": router_weights, "accepted": accepted, "parents": parents, "expert_weights": expert_weights}


def reference(tokens, route_ids, router_weights, accepted, parents, expert_weights):
    matches = route_ids[:, :, None] == jnp.arange(E_WIN, dtype=jnp.int32)[None, None, :]
    live_rows = accepted > 0
    combine = jnp.where(live_rows[:, None], jnp.sum(jnp.where(matches, router_weights[:, :, None], 0.0), axis=1), 0.0)

    def expert_step(summed, expert):
        matrices = expert_weights[expert]
        gate_part = jnp.dot(tokens, matrices[0].T, preferred_element_type=jnp.float32)
        up_part = jnp.dot(tokens, matrices[1].T, preferred_element_type=jnp.float32)
        factor = combine[:, expert]
        weighted = (factor[:, None] * jax.nn.silu(gate_part) * up_part).astype(jnp.bfloat16)
        produced = jnp.dot(weighted, matrices[2], preferred_element_type=jnp.float32)
        return summed + produced, jnp.zeros((), jnp.float32)

    start = jnp.zeros((ROWS, D), jnp.float32)
    summed, unused = lax.scan(expert_step, start, jnp.arange(E_WIN, dtype=jnp.int32))
    expert_out = summed.astype(jnp.bfloat16)
    tree_count = ROWS // NODES
    grouped = expert_out.reshape(tree_count, NODES, D)
    parent_out = grouped[jnp.arange(tree_count)[:, None], parents.reshape(tree_count, NODES)].reshape(ROWS, D)
    return expert_out, parent_out
```

```python
import functools

import jax
import jax.numpy as jnp
from jax import lax
from jax.experimental import pallas as pl
from jax.experimental.pallas import tpu as pltpu
from jax.sharding import PartitionSpec as P

NODES = 64
CAP = 32
MESH = pl.DeviceIdType.MESH


def moe_kernel(
    n, ids_ref, rw_ref, acc_ref, par_ref, tok_ref, w_hbm, out_ref, pout_ref,
    w, xsend, xbuf, psend, pbuf, hbuf, fsend, fin,
    w_sem, xs_sem, xr_sem, ps_sem, pr_sem, hs_sem, hr_sem, fs_sem, fr_sem,
):
    me = lax.axis_index("loop")
    hid = lax.axis_index("hid")
    rows, width = tok_ref.shape
    experts, _, share, slab = w.shape
    slots = experts * CAP
    on_diag = me == hid

    def plus(k):
        return lax.rem(me + k, n)

    def minus(k):
        return lax.rem(me + n - k, n)

    barrier = pltpu.get_barrier_semaphore()
    for k in range(1, n):
        pl.semaphore_signal(barrier, inc=1, device_id={"loop": plus(k)}, device_id_type=MESH)
    for k in range(1, n):
        pl.semaphore_signal(
            barrier, inc=1, device_id={"loop": hid, "hid": lax.rem(hid + k, n)}, device_id_type=MESH
        )

    @pl.when(jnp.logical_not(on_diag))
    def _():
        pl.semaphore_signal(barrier, inc=1, device_id={"loop": hid, "hid": hid}, device_id_type=MESH)

    w_copies = [pltpu.make_async_copy(w_hbm.at[e], w.at[e], w_sem.at[e]) for e in range(experts)]
    for copy in w_copies:
        copy.start()

    f32, bf16 = jnp.float32, jnp.bfloat16
    r_i = lax.broadcasted_iota(jnp.int32, (rows, rows), 0)
    c_i = lax.broadcasted_iota(jnp.int32, (rows, rows), 1)
    eye = r_i == c_i
    acc = jnp.sum(jnp.where(eye, acc_ref[...].astype(f32), 0.0), axis=1, keepdims=True)
    live = acc > 0.0
    ids = ids_ref[...]
    rw = rw_ref[...]
    lane = lax.broadcasted_iota(jnp.int32, (rows, slots), 1)
    lane_e = lane // CAP
    lane_i = (lane - lane_e * CAP).astype(f32)
    match = jnp.zeros((rows, slots), f32)
    factor = jnp.zeros((rows, slots), f32)
    for e in range(experts):
        hit = (ids == e) & live
        m_e = jnp.sum(jnp.where(hit, 1.0, 0.0), axis=1, keepdims=True)
        f_e = jnp.sum(jnp.where(hit, rw, 0.0), axis=1, keepdims=True)
        match = jnp.where(lane_e == e, m_e, match)
        factor = jnp.where(lane_e == e, f_e, factor)
    lower = jnp.where(c_i < r_i, 1.0, 0.0).astype(bf16)
    rank = jnp.dot(lower, match.astype(bf16), preferred_element_type=f32)
    picked = (match > 0.0) & (rank == lane_i)
    place = jnp.where(picked, 1.0, 0.0)
    place_t = jnp.transpose(place).astype(bf16)
    factor_row = jnp.sum(jnp.where(picked, factor, 0.0), axis=0, keepdims=True)
    s_r = lax.broadcasted_iota(jnp.int32, (slots, slots), 0)
    s_c = lax.broadcasted_iota(jnp.int32, (slots, slots), 1)
    factor_col = jnp.sum(jnp.where(s_r == s_c, factor_row, 0.0), axis=1, keepdims=True)

    for k in range(n):
        cols = pl.ds(pl.multiple_of(plus(k) * slab, slab), slab)
        chosen = jnp.dot(place_t, tok_ref[:, cols], preferred_element_type=f32).astype(bf16)
        target = xbuf if k == 0 else xsend
        target[k if k == 0 else k - 1] = chosen.reshape(experts, CAP, slab)

    @pl.when(on_diag)
    def _():
        pl.semaphore_wait(barrier, 2 * (n - 1))

    @pl.when(jnp.logical_not(on_diag))
    def _():
        pl.semaphore_wait(barrier, 2 * (n - 1) + 1)

    def x_copy(k, e):
        return pltpu.make_async_remote_copy(
            src_ref=xsend.at[k - 1, e], dst_ref=xbuf.at[k, e],
            send_sem=xs_sem.at[k - 1, e], recv_sem=xr_sem.at[k - 1, e],
            device_id={"loop": plus(k)}, device_id_type=MESH,
        )

    def p_copy(k, e):
        return pltpu.make_async_remote_copy(
            src_ref=psend.at[e, k], dst_ref=pbuf.at[k - 1, e],
            send_sem=ps_sem.at[k - 1, e], recv_sem=pr_sem.at[k - 1, e],
            device_id={"loop": minus(k)}, device_id_type=MESH,
        )

    def h_copy(k, e):
        return pltpu.make_async_remote_copy(
            src_ref=hbuf.at[e, 0], dst_ref=hbuf.at[e, k],
            send_sem=hs_sem.at[k - 1, e], recv_sem=hr_sem.at[k - 1, e],
            device_id={"loop": plus(k)}, device_id_type=MESH,
        )

    def f_copy(k, e, source):
        return pltpu.make_async_remote_copy(
            src_ref=fsend.at[e, k], dst_ref=fin.at[source, e],
            send_sem=fs_sem.at[k, e], recv_sem=fr_sem.at[source, e],
            device_id={"loop": minus(k), "hid": me}, device_id_type=MESH,
        )

    others = list(range(1, n))
    for e in range(experts):
        for k in others:
            x_copy(k, e).start()

    for e in range(experts):
        w_copies[e].wait()
        for k in others:
            x_copy(k, e).wait_recv()
        part = lax.dot_general(
            xbuf[:, e].reshape(n * CAP, slab), w[e, 0:2].reshape(2 * share, slab),
            (((1,), (1,)), ((), ())), preferred_element_type=f32,
        )
        psend[e] = part.reshape(n, CAP, 2 * share)
        for k in others:
            p_copy(k, e).start()

    for e in range(experts):
        for k in others:
            p_copy(k, e).wait_recv()
        total = psend[e, 0]
        for k in others:
            total = total + pbuf[k - 1, e]
        gate, up = total[:, :share], total[:, share:]
        col = factor_col[e * CAP:(e + 1) * CAP]
        hbuf[e, 0] = (col * (gate / (1.0 + jnp.exp(-gate))) * up).astype(bf16)
        for k in others:
            h_copy(k, e).start()

    for e in range(experts):
        for k in others:
            h_copy(k, e).wait_recv()
        block = jnp.dot(
            hbuf[e].reshape(n * CAP, share), w[e, 2], preferred_element_type=f32
        ).astype(bf16).reshape(n, CAP, slab)
        fsend[e] = block
        for k in others:
            f_copy(k, e, hid).start()

        @pl.when(on_diag)
        def _():
            fin[hid, e] = block[0]

        @pl.when(jnp.logical_not(on_diag))
        def _():
            f_copy(0, e, hid).start()

    base = r_i // NODES * NODES
    par = jnp.sum(jnp.where(eye, par_ref[...].astype(f32), 0.0), axis=1, keepdims=True)
    family = jnp.where((c_i - base).astype(f32) == par, 1.0, 0.0).astype(bf16)
    place16 = place.astype(bf16)

    for source in range(n):
        @pl.when(jnp.logical_not(on_diag & (hid == source)))
        def _():
            for e in range(experts):
                f_copy(1, e, source).wait_recv()

    total = fin[0].astype(f32)
    for source in range(1, n):
        total = total + fin[source].astype(f32)
    total = total.reshape(slots, slab)
    high = total.astype(bf16)
    low = (total - high.astype(f32)).astype(bf16)
    value = jnp.dot(place16, high, preferred_element_type=f32) + jnp.dot(
        place16, low, preferred_element_type=f32
    )
    value = value.astype(bf16)
    out_ref[...] = value
    pout_ref[...] = jnp.dot(family, value, preferred_element_type=f32).astype(bf16)

    for e in range(experts):
        for k in others:
            x_copy(k, e).wait_send()
            p_copy(k, e).wait_send()
            h_copy(k, e).wait_send()
            f_copy(k, e, hid).wait_send()

        @pl.when(jnp.logical_not(on_diag))
        def _():
            f_copy(0, e, hid).wait_send()


def compact(tokens, route_ids, router_weights, accepted, parents, expert_weights):
    n = lax.axis_size("loop")
    rows = tokens.shape[0]
    experts, _, share, slab = expert_weights.shape
    bf16, f32 = jnp.bfloat16, jnp.float32
    vmem = pl.BlockSpec(memory_space=pltpu.VMEM)
    dma = pltpu.SemaphoreType.DMA
    return pl.pallas_call(
        functools.partial(moe_kernel, n),
        out_shape=[jax.ShapeDtypeStruct((rows, slab), bf16)] * 2,
        in_specs=[vmem] * 5 + [pl.BlockSpec(memory_space=pl.ANY)],
        out_specs=[vmem] * 2,
        scratch_shapes=[
            pltpu.VMEM(expert_weights.shape, bf16),
            pltpu.VMEM((n - 1, experts, CAP, slab), bf16),
            pltpu.VMEM((n, experts, CAP, slab), bf16),
            pltpu.VMEM((experts, n, CAP, 2 * share), f32),
            pltpu.VMEM((n - 1, experts, CAP, 2 * share), f32),
            pltpu.VMEM((experts, n, CAP, share), bf16),
            pltpu.VMEM((experts, n, CAP, slab), bf16),
            pltpu.VMEM((n, experts, CAP, slab), bf16),
            dma((experts,)),
            dma((n - 1, experts)), dma((n - 1, experts)),
            dma((n - 1, experts)), dma((n - 1, experts)),
            dma((n - 1, experts)), dma((n - 1, experts)),
            dma((n, experts)), dma((n, experts)),
        ],
        compiler_params=pltpu.CompilerParams(
            collective_id=0, has_side_effects=True, vmem_limit_bytes=40 << 20
        ),
    )(route_ids, router_weights, accepted.reshape(1, rows), parents.reshape(1, rows), tokens, expert_weights)


def shifted(value, axis, by):
    devices = lax.axis_size(axis)
    return lax.ppermute(value, axis, [(i, (i + by) % devices) for i in range(devices)])


def move_one(piece, phase_name):
    if phase_name == "proj":
        return shifted(piece, "loop", 1)
    return shifted(piece, "loop", 1)


def rotate(piece, start_value, add_piece, phase_name):
    n_loop = lax.axis_size("loop")
    own_index = lax.axis_index("loop")
    total = add_piece(start_value, piece, own_index)

    def turn_body(turn_no, carried):
        arrived = move_one(carried[0], phase_name)
        anchor = jnp.mod(own_index - turn_no, n_loop)
        return (arrived, add_piece(carried[1], arrived, anchor))

    carried = lax.fori_loop(1, n_loop, turn_body, (piece, total))
    return carried[1]


def general(tokens, route_ids, router_weights, accepted, parents, expert_weights):
    row_count = tokens.shape[0]
    model_width = tokens.shape[1]
    window_count = expert_weights.shape[0]
    hidden_share = expert_weights.shape[2]
    slab_width = expert_weights.shape[3]
    proj_weights = expert_weights[:, 0:2]
    down_weights = expert_weights[:, 2]
    matches = route_ids[:, :, None] == jnp.arange(window_count, dtype=jnp.int32)[None, None, :]
    live_rows = accepted > 0
    combine = jnp.where(
        live_rows[:, None],
        jnp.sum(jnp.where(matches, router_weights[:, :, None], 0.0), axis=1),
        0.0,
    )

    def proj_piece(total, piece, anchor):
        columns = lax.dynamic_slice_in_dim(tokens, anchor * slab_width, slab_width, 1)
        return total + jnp.einsum(
            "rd,etfd->retf", columns, piece, preferred_element_type=jnp.float32
        )

    proj_start = jnp.zeros((row_count, window_count, 2, hidden_share), jnp.float32)
    projected = rotate(proj_weights, proj_start, proj_piece, "proj")
    weighted = (combine[:, :, None] * jax.nn.silu(projected[:, :, 0]) * projected[:, :, 1]).astype(
        jnp.bfloat16
    )

    def down_piece(total, piece, anchor):
        block = jnp.einsum("ref,efd->rd", weighted, piece, preferred_element_type=jnp.float32)
        return lax.dynamic_update_slice_in_dim(total, block, anchor * slab_width, 1)

    partial_value = rotate(
        down_weights, jnp.zeros((row_count, model_width), jnp.float32), down_piece, "down"
    )
    share_width = model_width // lax.axis_size("hid")
    summed_all = lax.psum(partial_value, "hid")
    expert_out = lax.dynamic_slice_in_dim(
        summed_all, lax.axis_index("hid") * share_width, share_width, 1
    ).astype(jnp.bfloat16)
    tree_count = row_count // NODES
    family = jax.nn.one_hot(parents.reshape(tree_count, NODES), NODES, dtype=jnp.bfloat16)
    grouped = expert_out.reshape(tree_count, NODES, share_width)
    parent_out = jnp.einsum("qnm,qmd->qnd", family, grouped, preferred_element_type=jnp.float32)
    parent_out = parent_out.astype(jnp.bfloat16).reshape(row_count, share_width)
    return (expert_out, parent_out)


def local(tokens, route_ids, router_weights, accepted, parents, expert_weights):
    args = (tokens, route_ids, router_weights, accepted, parents, expert_weights)
    experts, _, share, slab = expert_weights.shape
    n_loop, n_hid = lax.axis_size("loop"), lax.axis_size("hid")
    if n_loop == n_hid and slab % 128 == 0 and share % 128 == 0 and experts * CAP == 128:
        return tuple(compact(*args))
    return general(*args)


def solution(mesh):
    in_specs = (
        P(("groups", "loop"), None),
        P(("groups", "loop"), None),
        P(("groups", "loop"), None),
        P(("groups", "loop")),
        P(("groups", "loop")),
        P(None, None, "hid", "loop"),
    )
    out_specs = (P(("groups", "loop"), "hid"), P(("groups", "loop"), "hid"))
    return jax.shard_map(local, mesh=mesh, in_specs=in_specs, out_specs=out_specs, check_vma=False)
```

```python
import functools

import jax
import jax.numpy as jnp
from jax import lax
from jax.experimental import pallas as pl
from jax.experimental.pallas import tpu as pltpu
from jax.sharding import PartitionSpec as P

NODES = 64
CAP = 32
MESH = pl.DeviceIdType.MESH
SENT = jnp.bfloat16


def moe_kernel(
    n, ids_hbm, rw_hbm, acc_hbm, par_hbm, tok_hbm, w_hbm, out_ref, pout_ref,
    ids_ref, rw_ref, acc_ref, par_ref, tok_ref, w,
    xsend, xbuf, pown, psend, pbuf, hbuf, fsend, rbuf, tsend, fin,
    in_sem, w_sem, xs_sem, xf_sem, xr_sem, ps_sem, pr_sem, hs_sem, hr_sem,
    rs_sem, rr_sem, ts_sem, tr_sem,
):
    me = lax.axis_index("loop")
    hid = lax.axis_index("hid")
    rows, width = tok_ref.shape
    experts, _, share, slab = w.shape
    slots = experts * CAP
    on_diag = me == hid
    others = list(range(1, n))

    def plus(index, k):
        return lax.rem(index + k, n)

    def minus(index, k):
        return lax.rem(index + n - k, n)

    barrier = pltpu.get_barrier_semaphore()
    for k in others:
        pl.semaphore_signal(barrier, inc=1, device_id={"loop": plus(me, k)}, device_id_type=MESH)
        pl.semaphore_signal(barrier, inc=1, device_id={"hid": plus(hid, k)}, device_id_type=MESH)

    @pl.when(jnp.logical_not(on_diag))
    def _():
        pl.semaphore_signal(barrier, inc=1, device_id={"loop": hid, "hid": me}, device_id_type=MESH)

    inputs = [
        pltpu.make_async_copy(source, target, in_sem.at[i])
        for i, (source, target) in enumerate(
            [(ids_hbm, ids_ref), (rw_hbm, rw_ref), (acc_hbm, acc_ref), (par_hbm, par_ref), (tok_hbm, tok_ref)]
        )
    ]
    for copy in inputs:
        copy.start()
    w_copies = [pltpu.make_async_copy(w_hbm.at[e], w.at[e], w_sem.at[e]) for e in range(experts)]
    for copy in w_copies:
        copy.start()

    f32, bf16 = jnp.float32, jnp.bfloat16
    r_i = lax.broadcasted_iota(jnp.int32, (rows, rows), 0)
    c_i = lax.broadcasted_iota(jnp.int32, (rows, rows), 1)
    upper = jnp.where(r_i < c_i, 1.0, 0.0).astype(bf16)
    slot = lax.broadcasted_iota(jnp.int32, (slots, rows), 0)
    slot_e = slot // CAP
    slot_i = (slot - slot_e * CAP).astype(f32)
    for copy in inputs:
        copy.wait()
    live = acc_ref[...] > 0
    ids = ids_ref[...]
    rw = rw_ref[...]
    match = jnp.zeros((slots, rows), f32)
    factor = jnp.zeros((slots, rows), f32)
    for e in range(experts):
        hit = (ids == e) & live
        m_e = jnp.sum(jnp.where(hit, 1.0, 0.0), axis=0, keepdims=True)
        f_e = jnp.sum(jnp.where(hit, rw, 0.0), axis=0, keepdims=True)
        match = jnp.where(slot_e == e, m_e, match)
        factor = jnp.where(slot_e == e, f_e, factor)
    rank = jnp.dot(match.astype(bf16), upper, preferred_element_type=f32)
    picked = (match > 0.0) & (rank == slot_i)
    place_t = jnp.where(picked, 1.0, 0.0)
    factor_col = jnp.sum(jnp.where(picked, factor, 0.0), axis=1, keepdims=True)
    place_t16 = place_t.astype(bf16)

    for k in others + [0]:
        cols = pl.ds(pl.multiple_of(plus(me, k) * slab, slab), slab)
        chosen = jnp.dot(place_t16, tok_ref[:, cols], preferred_element_type=f32)
        chosen = chosen.astype(bf16).reshape(experts, CAP, slab)
        if k == 0:
            xbuf[0] = chosen
        else:
            xsend[k - 1] = chosen

    @pl.when(on_diag)
    def _():
        pl.semaphore_wait(barrier, 2 * (n - 1))

    @pl.when(jnp.logical_not(on_diag))
    def _():
        pl.semaphore_wait(barrier, 2 * (n - 1) + 1)

    def x_copy(k, e):
        return pltpu.make_async_remote_copy(
            src_ref=xsend.at[k - 1, e], dst_ref=xbuf.at[k, e],
            send_sem=xs_sem.at[k - 1], recv_sem=xr_sem.at[k - 1, e],
            device_id={"loop": plus(me, k)}, device_id_type=MESH,
        )

    def x_forward(k, j):
        return pltpu.make_async_remote_copy(
            src_ref=xbuf.at[k, hid], dst_ref=xbuf.at[k, hid],
            send_sem=xf_sem.at[k - 1, j - 1], recv_sem=xr_sem.at[k - 1, hid],
            device_id={"hid": plus(hid, j)}, device_id_type=MESH,
        )

    def p_copy(k, e):
        return pltpu.make_async_remote_copy(
            src_ref=psend.at[e, k - 1], dst_ref=pbuf.at[k - 1, e],
            send_sem=ps_sem.at[k - 1, e], recv_sem=pr_sem.at[k - 1, e],
            device_id={"loop": minus(me, k)}, device_id_type=MESH,
        )

    def h_copy(k, e):
        return pltpu.make_async_remote_copy(
            src_ref=hbuf.at[e, 0], dst_ref=hbuf.at[e, k],
            send_sem=hs_sem.at[k - 1, e], recv_sem=hr_sem.at[k - 1, e],
            device_id={"loop": plus(me, k)}, device_id_type=MESH,
        )

    def r_copy(j, e):
        return pltpu.make_async_remote_copy(
            src_ref=fsend.at[e, minus(me, plus(hid, j))], dst_ref=rbuf.at[j - 1, e],
            send_sem=rs_sem.at[j - 1, e], recv_sem=rr_sem.at[j - 1, e],
            device_id={"hid": plus(hid, j)}, device_id_type=MESH,
        )

    def t_copy(e):
        return pltpu.make_async_remote_copy(
            src_ref=tsend.at[e], dst_ref=fin.at[e],
            send_sem=ts_sem.at[e], recv_sem=tr_sem.at[e],
            device_id={"loop": hid, "hid": me}, device_id_type=MESH,
        )

    for k in others:
        x_copy(k, hid).start()
    for k in others:
        x_copy(k, hid).wait_recv()
        for j in others:
            x_forward(k, j).start()

    for e in range(experts):
        w_copies[e].wait()

        @pl.when(hid != e)
        def _():
            for k in others:
                x_copy(k, e).wait_recv()

        part = lax.dot_general(
            xbuf[:, e].reshape(n * CAP, slab), w[e, 0:2].reshape(2 * share, slab),
            (((1,), (1,)), ((), ())), preferred_element_type=f32,
        )
        pown[e] = part[:CAP]
        psend[e] = part[CAP:].astype(SENT).reshape(n - 1, CAP, 2 * share)
        for k in others:
            p_copy(k, e).start()

    for e in range(experts):
        for k in others:
            p_copy(k, e).wait_recv()
        total = pown[e]
        for k in others:
            total = total + pbuf[k - 1, e].astype(f32)
        gate, up = total[:, :share], total[:, share:]
        col = factor_col[e * CAP:(e + 1) * CAP]
        hbuf[e, 0] = (col * (gate / (1.0 + jnp.exp(-gate))) * up).astype(bf16)
        for k in others:
            h_copy(k, e).start()

    for e in range(experts):
        for k in others:
            h_copy(k, e).wait_recv()
        fsend[e] = jnp.dot(
            hbuf[e].reshape(n * CAP, share), w[e, 2], preferred_element_type=f32
        ).reshape(n, CAP, slab)
        for j in others:
            r_copy(j, e).start()

    par = par_ref[...]
    family_t = jnp.where(r_i == c_i // NODES * NODES + par, 1.0, 0.0)
    family = jnp.transpose(family_t).astype(bf16)
    place = jnp.transpose(place_t).astype(bf16)

    for e in range(experts):
        for j in others:
            r_copy(j, e).wait_recv()
        total = fsend[e, minus(me, hid)]
        for j in others:
            total = total + rbuf[j - 1, e]

        @pl.when(on_diag)
        def _():
            fin[e] = total.astype(bf16)

        @pl.when(jnp.logical_not(on_diag))
        def _():
            tsend[e] = total.astype(bf16)
            t_copy(e).start()

    @pl.when(jnp.logical_not(on_diag))
    def _():
        for e in range(experts):
            t_copy(e).wait_recv()

    value = jnp.dot(place, fin[...].reshape(slots, slab), preferred_element_type=f32).astype(bf16)
    out_ref[...] = value
    pout_ref[...] = jnp.dot(family, value, preferred_element_type=f32).astype(bf16)

    for k in others:
        x_copy(k, hid).wait_send()
        for j in others:
            x_forward(k, j).wait_send()
        for e in range(experts):
            p_copy(k, e).wait_send()
            h_copy(k, e).wait_send()
            r_copy(k, e).wait_send()

    @pl.when(jnp.logical_not(on_diag))
    def _():
        for e in range(experts):
            t_copy(e).wait_send()


def compact(tokens, route_ids, router_weights, accepted, parents, expert_weights):
    n = lax.axis_size("loop")
    rows = tokens.shape[0]
    experts, _, share, slab = expert_weights.shape
    bf16, f32 = jnp.bfloat16, jnp.float32
    vmem = pl.BlockSpec(memory_space=pltpu.VMEM)
    dma = pltpu.SemaphoreType.DMA
    args = (
        route_ids.T, router_weights.T, accepted.reshape(1, rows), parents.reshape(1, rows),
        tokens, expert_weights,
    )
    return pl.pallas_call(
        functools.partial(moe_kernel, n),
        out_shape=[jax.ShapeDtypeStruct((rows, slab), bf16)] * 2,
        in_specs=[pl.BlockSpec(memory_space=pltpu.HBM)] * 6,
        out_specs=[vmem] * 2,
        scratch_shapes=[pltpu.VMEM(a.shape, a.dtype) for a in args] + [
            pltpu.VMEM((n - 1, experts, CAP, slab), bf16),
            pltpu.VMEM((n, experts, CAP, slab), bf16),
            pltpu.VMEM((experts, CAP, 2 * share), f32),
            pltpu.VMEM((experts, n - 1, CAP, 2 * share), SENT),
            pltpu.VMEM((n - 1, experts, CAP, 2 * share), SENT),
            pltpu.VMEM((experts, n, CAP, share), bf16),
            pltpu.VMEM((experts, n, CAP, slab), f32),
            pltpu.VMEM((n - 1, experts, CAP, slab), f32),
            pltpu.VMEM((experts, CAP, slab), bf16),
            pltpu.VMEM((experts, CAP, slab), bf16),
            dma((5,)), dma((experts,)),
            dma((n - 1,)), dma((n - 1, n - 1)), dma((n - 1, experts)),
            dma((n - 1, experts)), dma((n - 1, experts)),
            dma((n - 1, experts)), dma((n - 1, experts)),
            dma((n - 1, experts)), dma((n - 1, experts)),
            dma((experts,)), dma((experts,)),
        ],
        compiler_params=pltpu.CompilerParams(
            collective_id=0, has_side_effects=True, vmem_limit_bytes=40 << 20
        ),
    )(*args)


def shifted(value, axis, by):
    devices = lax.axis_size(axis)
    return lax.ppermute(value, axis, [(i, (i + by) % devices) for i in range(devices)])


def move_one(piece, phase_name):
    if phase_name == "proj":
        return shifted(piece, "loop", 1)
    return shifted(piece, "loop", 1)


def rotate(piece, start_value, add_piece, phase_name):
    n_loop = lax.axis_size("loop")
    own_index = lax.axis_index("loop")
    total = add_piece(start_value, piece, own_index)

    def turn_body(turn_no, carried):
        arrived = move_one(carried[0], phase_name)
        anchor = jnp.mod(own_index - turn_no, n_loop)
        return (arrived, add_piece(carried[1], arrived, anchor))

    carried = lax.fori_loop(1, n_loop, turn_body, (piece, total))
    return carried[1]


def general(tokens, route_ids, router_weights, accepted, parents, expert_weights):
    row_count = tokens.shape[0]
    model_width = tokens.shape[1]
    window_count = expert_weights.shape[0]
    hidden_share = expert_weights.shape[2]
    slab_width = expert_weights.shape[3]
    proj_weights = expert_weights[:, 0:2]
    down_weights = expert_weights[:, 2]
    matches = route_ids[:, :, None] == jnp.arange(window_count, dtype=jnp.int32)[None, None, :]
    live_rows = accepted > 0
    combine = jnp.where(
        live_rows[:, None],
        jnp.sum(jnp.where(matches, router_weights[:, :, None], 0.0), axis=1),
        0.0,
    )

    def proj_piece(total, piece, anchor):
        columns = lax.dynamic_slice_in_dim(tokens, anchor * slab_width, slab_width, 1)
        return total + jnp.einsum(
            "rd,etfd->retf", columns, piece, preferred_element_type=jnp.float32
        )

    proj_start = jnp.zeros((row_count, window_count, 2, hidden_share), jnp.float32)
    projected = rotate(proj_weights, proj_start, proj_piece, "proj")
    weighted = (combine[:, :, None] * jax.nn.silu(projected[:, :, 0]) * projected[:, :, 1]).astype(
        jnp.bfloat16
    )

    def down_piece(total, piece, anchor):
        block = jnp.einsum("ref,efd->rd", weighted, piece, preferred_element_type=jnp.float32)
        return lax.dynamic_update_slice_in_dim(total, block, anchor * slab_width, 1)

    partial_value = rotate(
        down_weights, jnp.zeros((row_count, model_width), jnp.float32), down_piece, "down"
    )
    share_width = model_width // lax.axis_size("hid")
    summed_all = lax.psum(partial_value, "hid")
    expert_out = lax.dynamic_slice_in_dim(
        summed_all, lax.axis_index("hid") * share_width, share_width, 1
    ).astype(jnp.bfloat16)
    tree_count = row_count // NODES
    family = jax.nn.one_hot(parents.reshape(tree_count, NODES), NODES, dtype=jnp.bfloat16)
    grouped = expert_out.reshape(tree_count, NODES, share_width)
    parent_out = jnp.einsum("qnm,qmd->qnd", family, grouped, preferred_element_type=jnp.float32)
    parent_out = parent_out.astype(jnp.bfloat16).reshape(row_count, share_width)
    return (expert_out, parent_out)


def local(tokens, route_ids, router_weights, accepted, parents, expert_weights):
    args = (tokens, route_ids, router_weights, accepted, parents, expert_weights)
    experts, _, share, slab = expert_weights.shape
    n_loop, n_hid = lax.axis_size("loop"), lax.axis_size("hid")
    if n_loop == n_hid and slab % 128 == 0 and share % 128 == 0 and experts == n_hid:
        return tuple(compact(*args))
    return general(*args)


def solution(mesh):
    in_specs = (
        P(("groups", "loop"), None),
        P(("groups", "loop"), None),
        P(("groups", "loop"), None),
        P(("groups", "loop")),
        P(("groups", "loop")),
        P(None, None, "hid", "loop"),
    )
    out_specs = (P(("groups", "loop"), "hid"), P(("groups", "loop"), "hid"))
    return jax.shard_map(local, mesh=mesh, in_specs=in_specs, out_specs=out_specs, check_vma=False)
```

```python
import functools

import jax
import jax.numpy as jnp
from jax import lax
from jax.experimental import pallas as pl
from jax.experimental.pallas import tpu as pltpu
from jax.sharding import PartitionSpec as P

NODES = 64
CAP = 32
MESH = pl.DeviceIdType.MESH
SENT = jnp.bfloat16


def moe_kernel(
    n, ids_hbm, rw_hbm, acc_hbm, par_hbm, tok_hbm, w_hbm, out_ref, pout_ref,
    ids_ref, rw_ref, acc_ref, par_ref, tok_ref, w,
    xsend, xbuf, pown, psend, pbuf, hbuf, fsend, rbuf, tsend, fin,
    in_sem, w_sem, xs_sem, xf_sem, xr_sem, ps_sem, pr_sem, hs_sem, hr_sem,
    rs_sem, rr_sem, ts_sem, tr_sem,
):
    me = lax.axis_index("loop")
    hid = lax.axis_index("hid")
    rows, width = tok_ref.shape
    experts, _, share, slab = w.shape
    slots = experts * CAP
    on_diag = me == hid
    others = list(range(1, n))

    def plus(index, k):
        return lax.rem(index + k, n)

    def minus(index, k):
        return lax.rem(index + n - k, n)

    barrier = pltpu.get_barrier_semaphore()
    for k in others:
        pl.semaphore_signal(barrier, inc=1, device_id={"loop": plus(me, k)}, device_id_type=MESH)
        pl.semaphore_signal(barrier, inc=1, device_id={"hid": plus(hid, k)}, device_id_type=MESH)

    @pl.when(jnp.logical_not(on_diag))
    def _():
        pl.semaphore_signal(barrier, inc=1, device_id={"loop": hid, "hid": me}, device_id_type=MESH)

    inputs = [
        pltpu.make_async_copy(source, target, in_sem.at[i])
        for i, (source, target) in enumerate(
            [(ids_hbm, ids_ref), (rw_hbm, rw_ref), (acc_hbm, acc_ref), (par_hbm, par_ref), (tok_hbm, tok_ref)]
        )
    ]
    for copy in inputs:
        copy.start()
    w_copies = [pltpu.make_async_copy(w_hbm.at[e], w.at[e], w_sem.at[e]) for e in range(experts)]
    for copy in w_copies:
        copy.start()

    f32, bf16 = jnp.float32, jnp.bfloat16
    r_i = lax.broadcasted_iota(jnp.int32, (rows, rows), 0)
    c_i = lax.broadcasted_iota(jnp.int32, (rows, rows), 1)
    upper = jnp.where(r_i < c_i, 1.0, 0.0).astype(bf16)
    slot = lax.broadcasted_iota(jnp.int32, (slots, rows), 0)
    slot_e = slot // CAP
    slot_i = (slot - slot_e * CAP).astype(f32)
    for copy in inputs:
        copy.wait()
    live = acc_ref[...] > 0
    ids = ids_ref[...]
    rw = rw_ref[...]
    match = jnp.zeros((slots, rows), f32)
    factor = jnp.zeros((slots, rows), f32)
    for e in range(experts):
        hit = (ids == e) & live
        m_e = jnp.sum(jnp.where(hit, 1.0, 0.0), axis=0, keepdims=True)
        f_e = jnp.sum(jnp.where(hit, rw, 0.0), axis=0, keepdims=True)
        match = jnp.where(slot_e == e, m_e, match)
        factor = jnp.where(slot_e == e, f_e, factor)
    rank = jnp.dot(match.astype(bf16), upper, preferred_element_type=f32)
    picked = (match > 0.0) & (rank == slot_i)
    place_t = jnp.where(picked, 1.0, 0.0)
    factor_col = jnp.sum(jnp.where(picked, factor, 0.0), axis=1, keepdims=True)
    place_t16 = place_t.astype(bf16)

    for k in others + [0]:
        cols = pl.ds(pl.multiple_of(plus(me, k) * slab, slab), slab)
        chosen = jnp.dot(place_t16, tok_ref[:, cols], preferred_element_type=f32)
        chosen = chosen.astype(bf16).reshape(experts, CAP, slab)
        if k == 0:
            xbuf[0] = chosen
        else:
            xsend[k - 1] = chosen

    @pl.when(on_diag)
    def _():
        pl.semaphore_wait(barrier, 2 * (n - 1))

    @pl.when(jnp.logical_not(on_diag))
    def _():
        pl.semaphore_wait(barrier, 2 * (n - 1) + 1)

    def x_copy(k, e):
        return pltpu.make_async_remote_copy(
            src_ref=xsend.at[k - 1, e], dst_ref=xbuf.at[k, e],
            send_sem=xs_sem.at[k - 1], recv_sem=xr_sem.at[k - 1, e],
            device_id={"loop": plus(me, k)}, device_id_type=MESH,
        )

    def x_forward(k, j):
        return pltpu.make_async_remote_copy(
            src_ref=xbuf.at[k, hid], dst_ref=xbuf.at[k, hid],
            send_sem=xf_sem.at[k - 1, j - 1], recv_sem=xr_sem.at[k - 1, hid],
            device_id={"hid": plus(hid, j)}, device_id_type=MESH,
        )

    def p_copy(k, e):
        return pltpu.make_async_remote_copy(
            src_ref=psend.at[e, k - 1], dst_ref=pbuf.at[k - 1, e],
            send_sem=ps_sem.at[k - 1, e], recv_sem=pr_sem.at[k - 1, e],
            device_id={"loop": minus(me, k)}, device_id_type=MESH,
        )

    def h_copy(k, e):
        return pltpu.make_async_remote_copy(
            src_ref=hbuf.at[e, 0], dst_ref=hbuf.at[e, k],
            send_sem=hs_sem.at[k - 1, e], recv_sem=hr_sem.at[k - 1, e],
            device_id={"loop": plus(me, k)}, device_id_type=MESH,
        )

    def r_copy(j, e):
        return pltpu.make_async_remote_copy(
            src_ref=fsend.at[e, minus(me, plus(hid, j))], dst_ref=rbuf.at[j - 1, e],
            send_sem=rs_sem.at[j - 1, e], recv_sem=rr_sem.at[j - 1, e],
            device_id={"hid": plus(hid, j)}, device_id_type=MESH,
        )

    def t_copy(e):
        return pltpu.make_async_remote_copy(
            src_ref=tsend.at[e], dst_ref=fin.at[e],
            send_sem=ts_sem.at[e], recv_sem=tr_sem.at[e],
            device_id={"loop": hid, "hid": me}, device_id_type=MESH,
        )

    for k in others:
        x_copy(k, hid).start()
    for k in others:
        x_copy(k, hid).wait_recv()
        for j in others:
            x_forward(k, j).start()

    def project(e):
        w_copies[e].wait()

        @pl.when(hid != e)
        def _():
            for k in others:
                x_copy(k, e).wait_recv()

        part = lax.dot_general(
            xbuf[:, e].reshape(n * CAP, slab), w[e, 0:2].reshape(2 * share, slab),
            (((1,), (1,)), ((), ())), preferred_element_type=f32,
        )
        pown[e] = part[:CAP]
        psend[e] = part[CAP:].astype(SENT).reshape(n - 1, CAP, 2 * share)
        for k in others:
            p_copy(k, e).start()

    def activate(e):
        for k in others:
            p_copy(k, e).wait_recv()
        total = pown[e]
        for k in others:
            total = total + pbuf[k - 1, e].astype(f32)
        gate, up = total[:, :share], total[:, share:]
        col = factor_col[e * CAP:(e + 1) * CAP]
        hbuf[e, 0] = (col * (gate / (1.0 + jnp.exp(-gate))) * up).astype(bf16)
        for k in others:
            h_copy(k, e).start()

    def down(e):
        for k in others:
            h_copy(k, e).wait_recv()
        fsend[e] = jnp.dot(
            hbuf[e].reshape(n * CAP, share), w[e, 2], preferred_element_type=f32
        ).reshape(n, CAP, slab)
        for j in others:
            r_copy(j, e).start()

    def collect(e):
        for j in others:
            r_copy(j, e).wait_recv()
        total = fsend[e, minus(me, hid)]
        for j in others:
            total = total + rbuf[j - 1, e]

        @pl.when(on_diag)
        def _():
            fin[e] = total.astype(bf16)

        @pl.when(jnp.logical_not(on_diag))
        def _():
            tsend[e] = total.astype(bf16)
            t_copy(e).start()

    project(0)
    par = par_ref[...]
    family_t = jnp.where(r_i == c_i // NODES * NODES + par, 1.0, 0.0)
    family = jnp.transpose(family_t).astype(bf16)
    place = jnp.transpose(place_t).astype(bf16)
    for turn in range(experts + 2):
        if turn + 1 < experts:
            project(turn + 1)
        if turn < experts:
            activate(turn)
        if 0 <= turn - 1 < experts:
            down(turn - 1)
        if 0 <= turn - 2 < experts:
            collect(turn - 2)

    @pl.when(jnp.logical_not(on_diag))
    def _():
        for e in range(experts):
            t_copy(e).wait_recv()

    value = jnp.dot(place, fin[...].reshape(slots, slab), preferred_element_type=f32).astype(bf16)
    out_ref[...] = value
    pout_ref[...] = jnp.dot(family, value, preferred_element_type=f32).astype(bf16)

    for k in others:
        x_copy(k, hid).wait_send()
        for j in others:
            x_forward(k, j).wait_send()
        for e in range(experts):
            p_copy(k, e).wait_send()
            h_copy(k, e).wait_send()
            r_copy(k, e).wait_send()

    @pl.when(jnp.logical_not(on_diag))
    def _():
        for e in range(experts):
            t_copy(e).wait_send()


def compact(tokens, route_ids, router_weights, accepted, parents, expert_weights):
    n = lax.axis_size("loop")
    rows = tokens.shape[0]
    experts, _, share, slab = expert_weights.shape
    bf16, f32 = jnp.bfloat16, jnp.float32
    vmem = pl.BlockSpec(memory_space=pltpu.VMEM)
    dma = pltpu.SemaphoreType.DMA
    args = (
        route_ids.T, router_weights.T, accepted.reshape(1, rows), parents.reshape(1, rows),
        tokens, expert_weights,
    )
    return pl.pallas_call(
        functools.partial(moe_kernel, n),
        out_shape=[jax.ShapeDtypeStruct((rows, slab), bf16)] * 2,
        in_specs=[pl.BlockSpec(memory_space=pltpu.HBM)] * 6,
        out_specs=[vmem] * 2,
        scratch_shapes=[pltpu.VMEM(a.shape, a.dtype) for a in args] + [
            pltpu.VMEM((n - 1, experts, CAP, slab), bf16),
            pltpu.VMEM((n, experts, CAP, slab), bf16),
            pltpu.VMEM((experts, CAP, 2 * share), f32),
            pltpu.VMEM((experts, n - 1, CAP, 2 * share), SENT),
            pltpu.VMEM((n - 1, experts, CAP, 2 * share), SENT),
            pltpu.VMEM((experts, n, CAP, share), bf16),
            pltpu.VMEM((experts, n, CAP, slab), f32),
            pltpu.VMEM((n - 1, experts, CAP, slab), f32),
            pltpu.VMEM((experts, CAP, slab), bf16),
            pltpu.VMEM((experts, CAP, slab), bf16),
            dma((5,)), dma((experts,)),
            dma((n - 1,)), dma((n - 1, n - 1)), dma((n - 1, experts)),
            dma((n - 1, experts)), dma((n - 1, experts)),
            dma((n - 1, experts)), dma((n - 1, experts)),
            dma((n - 1, experts)), dma((n - 1, experts)),
            dma((experts,)), dma((experts,)),
        ],
        compiler_params=pltpu.CompilerParams(
            collective_id=0, has_side_effects=True, vmem_limit_bytes=60 << 20
        ),
    )(*args)


def shifted(value, axis, by):
    devices = lax.axis_size(axis)
    return lax.ppermute(value, axis, [(i, (i + by) % devices) for i in range(devices)])


def move_one(piece, phase_name):
    if phase_name == "proj":
        return shifted(piece, "loop", 1)
    return shifted(piece, "loop", 1)


def rotate(piece, start_value, add_piece, phase_name):
    n_loop = lax.axis_size("loop")
    own_index = lax.axis_index("loop")
    total = add_piece(start_value, piece, own_index)

    def turn_body(turn_no, carried):
        arrived = move_one(carried[0], phase_name)
        anchor = jnp.mod(own_index - turn_no, n_loop)
        return (arrived, add_piece(carried[1], arrived, anchor))

    carried = lax.fori_loop(1, n_loop, turn_body, (piece, total))
    return carried[1]


def general(tokens, route_ids, router_weights, accepted, parents, expert_weights):
    row_count = tokens.shape[0]
    model_width = tokens.shape[1]
    window_count = expert_weights.shape[0]
    hidden_share = expert_weights.shape[2]
    slab_width = expert_weights.shape[3]
    proj_weights = expert_weights[:, 0:2]
    down_weights = expert_weights[:, 2]
    matches = route_ids[:, :, None] == jnp.arange(window_count, dtype=jnp.int32)[None, None, :]
    live_rows = accepted > 0
    combine = jnp.where(
        live_rows[:, None],
        jnp.sum(jnp.where(matches, router_weights[:, :, None], 0.0), axis=1),
        0.0,
    )

    def proj_piece(total, piece, anchor):
        columns = lax.dynamic_slice_in_dim(tokens, anchor * slab_width, slab_width, 1)
        return total + jnp.einsum(
            "rd,etfd->retf", columns, piece, preferred_element_type=jnp.float32
        )

    proj_start = jnp.zeros((row_count, window_count, 2, hidden_share), jnp.float32)
    projected = rotate(proj_weights, proj_start, proj_piece, "proj")
    weighted = (combine[:, :, None] * jax.nn.silu(projected[:, :, 0]) * projected[:, :, 1]).astype(
        jnp.bfloat16
    )

    def down_piece(total, piece, anchor):
        block = jnp.einsum("ref,efd->rd", weighted, piece, preferred_element_type=jnp.float32)
        return lax.dynamic_update_slice_in_dim(total, block, anchor * slab_width, 1)

    partial_value = rotate(
        down_weights, jnp.zeros((row_count, model_width), jnp.float32), down_piece, "down"
    )
    share_width = model_width // lax.axis_size("hid")
    summed_all = lax.psum(partial_value, "hid")
    expert_out = lax.dynamic_slice_in_dim(
        summed_all, lax.axis_index("hid") * share_width, share_width, 1
    ).astype(jnp.bfloat16)
    tree_count = row_count // NODES
    family = jax.nn.one_hot(parents.reshape(tree_count, NODES), NODES, dtype=jnp.bfloat16)
    grouped = expert_out.reshape(tree_count, NODES, share_width)
    parent_out = jnp.einsum("qnm,qmd->qnd", family, grouped, preferred_element_type=jnp.float32)
    parent_out = parent_out.astype(jnp.bfloat16).reshape(row_count, share_width)
    return (expert_out, parent_out)


def local(tokens, route_ids, router_weights, accepted, parents, expert_weights):
    args = (tokens, route_ids, router_weights, accepted, parents, expert_weights)
    experts, _, share, slab = expert_weights.shape
    n_loop, n_hid = lax.axis_size("loop"), lax.axis_size("hid")
    if n_loop == n_hid and slab % 128 == 0 and share % 128 == 0 and experts == n_hid:
        return tuple(compact(*args))
    return general(*args)


def solution(mesh):
    in_specs = (
        P(("groups", "loop"), None),
        P(("groups", "loop"), None),
        P(("groups", "loop"), None),
        P(("groups", "loop")),
        P(("groups", "loop")),
        P(None, None, "hid", "loop"),
    )
    out_specs = (P(("groups", "loop"), "hid"), P(("groups", "loop"), "hid"))
    return jax.shard_map(local, mesh=mesh, in_specs=in_specs, out_specs=out_specs, check_vma=False)
```

```python
import functools

import jax
import jax.numpy as jnp
from jax import lax
from jax.experimental import pallas as pl
from jax.experimental.pallas import tpu as pltpu
from jax.sharding import PartitionSpec as P

NODES = 64
CAP = 32
MESH = pl.DeviceIdType.MESH
SENT = jnp.bfloat16


def moe_kernel(
    n, ids_hbm, rw_hbm, acc_hbm, tok_hbm, w_hbm, sums_ref, place_ref,
    ids_ref, rw_ref, acc_ref, tok_ref, w,
    xsend, xbuf, pown, psend, pbuf, hbuf, fsend, rbuf, tsend, fin,
    in_sem, w_sem, xs_sem, xf_sem, xr_sem, ps_sem, pr_sem, hs_sem, hr_sem,
    rs_sem, rr_sem, ts_sem, tr_sem,
):
    me = lax.axis_index("loop")
    hid = lax.axis_index("hid")
    rows, width = tok_ref.shape
    experts, _, share, slab = w.shape
    slots = experts * CAP
    on_diag = me == hid
    others = list(range(1, n))

    def plus(index, k):
        return lax.rem(index + k, n)

    def minus(index, k):
        return lax.rem(index + n - k, n)

    barrier = pltpu.get_barrier_semaphore()
    for k in others:
        pl.semaphore_signal(barrier, inc=1, device_id={"loop": plus(me, k)}, device_id_type=MESH)
        pl.semaphore_signal(barrier, inc=1, device_id={"hid": plus(hid, k)}, device_id_type=MESH)

    @pl.when(jnp.logical_not(on_diag))
    def _():
        pl.semaphore_signal(barrier, inc=1, device_id={"loop": hid, "hid": me}, device_id_type=MESH)

    inputs = [
        pltpu.make_async_copy(source, target, in_sem.at[i])
        for i, (source, target) in enumerate(
            [(ids_hbm, ids_ref), (rw_hbm, rw_ref), (acc_hbm, acc_ref), (tok_hbm, tok_ref)]
        )
    ]
    for copy in inputs:
        copy.start()
    w_copies = [pltpu.make_async_copy(w_hbm.at[e], w.at[e], w_sem.at[e]) for e in range(experts)]
    for copy in w_copies:
        copy.start()

    f32, bf16 = jnp.float32, jnp.bfloat16
    r_i = lax.broadcasted_iota(jnp.int32, (rows, rows), 0)
    c_i = lax.broadcasted_iota(jnp.int32, (rows, rows), 1)
    upper = jnp.where(r_i < c_i, 1.0, 0.0).astype(bf16)
    slot = lax.broadcasted_iota(jnp.int32, (slots, rows), 0)
    slot_e = slot // CAP
    slot_i = (slot - slot_e * CAP).astype(f32)
    for copy in inputs:
        copy.wait()
    live = acc_ref[...] > 0
    ids = ids_ref[...]
    rw = rw_ref[...]
    match = jnp.zeros((slots, rows), f32)
    factor = jnp.zeros((slots, rows), f32)
    for e in range(experts):
        hit = (ids == e) & live
        m_e = jnp.sum(jnp.where(hit, 1.0, 0.0), axis=0, keepdims=True)
        f_e = jnp.sum(jnp.where(hit, rw, 0.0), axis=0, keepdims=True)
        match = jnp.where(slot_e == e, m_e, match)
        factor = jnp.where(slot_e == e, f_e, factor)
    rank = jnp.dot(match.astype(bf16), upper, preferred_element_type=f32)
    picked = (match > 0.0) & (rank == slot_i)
    place_t = jnp.where(picked, 1.0, 0.0)
    factor_col = jnp.sum(jnp.where(picked, factor, 0.0), axis=1, keepdims=True)
    place_t16 = place_t.astype(bf16)

    for k in others + [0]:
        cols = pl.ds(pl.multiple_of(plus(me, k) * slab, slab), slab)
        chosen = jnp.dot(place_t16, tok_ref[:, cols], preferred_element_type=f32)
        chosen = chosen.astype(bf16).reshape(experts, CAP, slab)
        if k == 0:
            xbuf[0] = chosen
        else:
            xsend[k - 1] = chosen

    @pl.when(on_diag)
    def _():
        pl.semaphore_wait(barrier, 2 * (n - 1))

    @pl.when(jnp.logical_not(on_diag))
    def _():
        pl.semaphore_wait(barrier, 2 * (n - 1) + 1)

    def x_copy(k, e):
        return pltpu.make_async_remote_copy(
            src_ref=xsend.at[k - 1, e], dst_ref=xbuf.at[k, e],
            send_sem=xs_sem.at[k - 1], recv_sem=xr_sem.at[k - 1, e],
            device_id={"loop": plus(me, k)}, device_id_type=MESH,
        )

    def x_forward(k, j):
        return pltpu.make_async_remote_copy(
            src_ref=xbuf.at[k, hid], dst_ref=xbuf.at[k, hid],
            send_sem=xf_sem.at[k - 1, j - 1], recv_sem=xr_sem.at[k - 1, hid],
            device_id={"hid": plus(hid, j)}, device_id_type=MESH,
        )

    def p_copy(k, e):
        return pltpu.make_async_remote_copy(
            src_ref=psend.at[e, k - 1], dst_ref=pbuf.at[k - 1, e],
            send_sem=ps_sem.at[k - 1, e], recv_sem=pr_sem.at[k - 1, e],
            device_id={"loop": minus(me, k)}, device_id_type=MESH,
        )

    def h_copy(k, e):
        return pltpu.make_async_remote_copy(
            src_ref=hbuf.at[e, 0], dst_ref=hbuf.at[e, k],
            send_sem=hs_sem.at[k - 1, e], recv_sem=hr_sem.at[k - 1, e],
            device_id={"loop": plus(me, k)}, device_id_type=MESH,
        )

    def r_copy(j, e):
        return pltpu.make_async_remote_copy(
            src_ref=fsend.at[e, minus(me, plus(hid, j))], dst_ref=rbuf.at[j - 1, e],
            send_sem=rs_sem.at[j - 1, e], recv_sem=rr_sem.at[j - 1, e],
            device_id={"hid": plus(hid, j)}, device_id_type=MESH,
        )

    def t_copy(e):
        return pltpu.make_async_remote_copy(
            src_ref=tsend.at[e], dst_ref=fin.at[e],
            send_sem=ts_sem.at[e], recv_sem=tr_sem.at[e],
            device_id={"loop": hid, "hid": me}, device_id_type=MESH,
        )

    for k in others:
        x_copy(k, hid).start()
    for k in others:
        x_copy(k, hid).wait_recv()
        for j in others:
            x_forward(k, j).start()

    def project(e):
        pltpu.make_async_copy(w_hbm.at[e], w.at[e], w_sem.at[e]).wait()
        part = lax.dot_general(
            xbuf[:, e].reshape(n * CAP, slab), w[e, 0:2].reshape(2 * share, slab),
            (((1,), (1,)), ((), ())), preferred_element_type=f32,
        )
        pown[e] = part[:CAP]
        psend[e] = part[CAP:].astype(SENT).reshape(n - 1, CAP, 2 * share)
        for k in others:
            p_copy(k, e).start()

    def project_other(e):
        @pl.when(hid != e)
        def _():
            for k in others:
                x_copy(k, e).wait_recv()
            project(e)

    def activate(e):
        for k in others:
            p_copy(k, e).wait_recv()
        total = pown[e]
        for k in others:
            total = total + pbuf[k - 1, e].astype(f32)
        gate, up = total[:, :share], total[:, share:]
        col = factor_col[e * CAP:(e + 1) * CAP]
        hbuf[e, 0] = (col * (gate / (1.0 + jnp.exp(-gate))) * up).astype(bf16)
        for k in others:
            h_copy(k, e).start()

    def down(e):
        for k in others:
            h_copy(k, e).wait_recv()
        fsend[e] = jnp.dot(
            hbuf[e].reshape(n * CAP, share), w[e, 2], preferred_element_type=f32
        ).reshape(n, CAP, slab)
        for j in others:
            r_copy(j, e).start()

    def collect(e):
        for j in others:
            r_copy(j, e).wait_recv()
        total = fsend[e, minus(me, hid)]
        for j in others:
            total = total + rbuf[j - 1, e]

        @pl.when(on_diag)
        def _():
            fin[e] = total.astype(bf16)

        @pl.when(jnp.logical_not(on_diag))
        def _():
            tsend[e] = total.astype(bf16)
            t_copy(e).start()

    project(hid)
    project_other(0)
    place_ref[...] = jnp.transpose(place_t).astype(bf16)
    for turn in range(experts + 2):
        if turn + 1 < experts:
            project_other(turn + 1)
        if turn < experts:
            activate(turn)
        if 0 <= turn - 1 < experts:
            down(turn - 1)
        if 0 <= turn - 2 < experts:
            collect(turn - 2)

    @pl.when(jnp.logical_not(on_diag))
    def _():
        for e in range(experts):
            t_copy(e).wait_recv()

    sums_ref[...] = fin[...].reshape(slots, slab)

    for k in others:
        x_copy(k, hid).wait_send()
        for j in others:
            x_forward(k, j).wait_send()
        for e in range(experts):
            p_copy(k, e).wait_send()
            h_copy(k, e).wait_send()
            r_copy(k, e).wait_send()

    @pl.when(jnp.logical_not(on_diag))
    def _():
        for e in range(experts):
            t_copy(e).wait_send()


def rows_kernel(sums_ref, place_ref, par_ref, out_ref, pout_ref):
    rows = place_ref.shape[0]
    f32, bf16 = jnp.float32, jnp.bfloat16
    r_i = lax.broadcasted_iota(jnp.int32, (rows, rows), 0)
    c_i = lax.broadcasted_iota(jnp.int32, (rows, rows), 1)
    family_t = jnp.where(r_i == c_i // NODES * NODES + par_ref[...], 1.0, 0.0)
    family = jnp.transpose(family_t).astype(bf16)
    value = jnp.dot(place_ref[...], sums_ref[...], preferred_element_type=f32).astype(bf16)
    out_ref[...] = value
    pout_ref[...] = jnp.dot(family, value, preferred_element_type=f32).astype(bf16)


def compact(tokens, route_ids, router_weights, accepted, parents, expert_weights):
    n = lax.axis_size("loop")
    rows = tokens.shape[0]
    experts, _, share, slab = expert_weights.shape
    bf16, f32 = jnp.bfloat16, jnp.float32
    vmem = pl.BlockSpec(memory_space=pltpu.VMEM)
    dma = pltpu.SemaphoreType.DMA
    args = (
        route_ids.T, router_weights.T, accepted.reshape(1, rows),
        tokens, expert_weights,
    )
    sums, place = pl.pallas_call(
        functools.partial(moe_kernel, n),
        out_shape=[
            jax.ShapeDtypeStruct((experts * CAP, slab), bf16),
            jax.ShapeDtypeStruct((rows, experts * CAP), bf16),
        ],
        in_specs=[pl.BlockSpec(memory_space=pltpu.HBM)] * 5,
        out_specs=[vmem] * 2,
        scratch_shapes=[pltpu.VMEM(a.shape, a.dtype) for a in args] + [
            pltpu.VMEM((n - 1, experts, CAP, slab), bf16),
            pltpu.VMEM((n, experts, CAP, slab), bf16),
            pltpu.VMEM((experts, CAP, 2 * share), f32),
            pltpu.VMEM((experts, n - 1, CAP, 2 * share), SENT),
            pltpu.VMEM((n - 1, experts, CAP, 2 * share), SENT),
            pltpu.VMEM((experts, n, CAP, share), bf16),
            pltpu.VMEM((experts, n, CAP, slab), f32),
            pltpu.VMEM((n - 1, experts, CAP, slab), f32),
            pltpu.VMEM((experts, CAP, slab), bf16),
            pltpu.VMEM((experts, CAP, slab), bf16),
            dma((4,)), dma((experts,)),
            dma((n - 1,)), dma((n - 1, n - 1)), dma((n - 1, experts)),
            dma((n - 1, experts)), dma((n - 1, experts)),
            dma((n - 1, experts)), dma((n - 1, experts)),
            dma((n - 1, experts)), dma((n - 1, experts)),
            dma((experts,)), dma((experts,)),
        ],
        compiler_params=pltpu.CompilerParams(
            collective_id=0, has_side_effects=True, vmem_limit_bytes=60 << 20
        ),
    )(*args)
    return pl.pallas_call(
        rows_kernel,
        out_shape=[jax.ShapeDtypeStruct((rows, slab), bf16)] * 2,
        in_specs=[vmem] * 3,
        out_specs=[vmem] * 2,
    )(sums, place, parents.reshape(1, rows))


def shifted(value, axis, by):
    devices = lax.axis_size(axis)
    return lax.ppermute(value, axis, [(i, (i + by) % devices) for i in range(devices)])


def move_one(piece, phase_name):
    if phase_name == "proj":
        return shifted(piece, "loop", 1)
    return shifted(piece, "loop", 1)


def rotate(piece, start_value, add_piece, phase_name):
    n_loop = lax.axis_size("loop")
    own_index = lax.axis_index("loop")
    total = add_piece(start_value, piece, own_index)

    def turn_body(turn_no, carried):
        arrived = move_one(carried[0], phase_name)
        anchor = jnp.mod(own_index - turn_no, n_loop)
        return (arrived, add_piece(carried[1], arrived, anchor))

    carried = lax.fori_loop(1, n_loop, turn_body, (piece, total))
    return carried[1]


def general(tokens, route_ids, router_weights, accepted, parents, expert_weights):
    row_count = tokens.shape[0]
    model_width = tokens.shape[1]
    window_count = expert_weights.shape[0]
    hidden_share = expert_weights.shape[2]
    slab_width = expert_weights.shape[3]
    proj_weights = expert_weights[:, 0:2]
    down_weights = expert_weights[:, 2]
    matches = route_ids[:, :, None] == jnp.arange(window_count, dtype=jnp.int32)[None, None, :]
    live_rows = accepted > 0
    combine = jnp.where(
        live_rows[:, None],
        jnp.sum(jnp.where(matches, router_weights[:, :, None], 0.0), axis=1),
        0.0,
    )

    def proj_piece(total, piece, anchor):
        columns = lax.dynamic_slice_in_dim(tokens, anchor * slab_width, slab_width, 1)
        return total + jnp.einsum(
            "rd,etfd->retf", columns, piece, preferred_element_type=jnp.float32
        )

    proj_start = jnp.zeros((row_count, window_count, 2, hidden_share), jnp.float32)
    projected = rotate(proj_weights, proj_start, proj_piece, "proj")
    weighted = (combine[:, :, None] * jax.nn.silu(projected[:, :, 0]) * projected[:, :, 1]).astype(
        jnp.bfloat16
    )

    def down_piece(total, piece, anchor):
        block = jnp.einsum("ref,efd->rd", weighted, piece, preferred_element_type=jnp.float32)
        return lax.dynamic_update_slice_in_dim(total, block, anchor * slab_width, 1)

    partial_value = rotate(
        down_weights, jnp.zeros((row_count, model_width), jnp.float32), down_piece, "down"
    )
    share_width = model_width // lax.axis_size("hid")
    summed_all = lax.psum(partial_value, "hid")
    expert_out = lax.dynamic_slice_in_dim(
        summed_all, lax.axis_index("hid") * share_width, share_width, 1
    ).astype(jnp.bfloat16)
    tree_count = row_count // NODES
    family = jax.nn.one_hot(parents.reshape(tree_count, NODES), NODES, dtype=jnp.bfloat16)
    grouped = expert_out.reshape(tree_count, NODES, share_width)
    parent_out = jnp.einsum("qnm,qmd->qnd", family, grouped, preferred_element_type=jnp.float32)
    parent_out = parent_out.astype(jnp.bfloat16).reshape(row_count, share_width)
    return (expert_out, parent_out)


def local(tokens, route_ids, router_weights, accepted, parents, expert_weights):
    args = (tokens, route_ids, router_weights, accepted, parents, expert_weights)
    experts, _, share, slab = expert_weights.shape
    n_loop, n_hid = lax.axis_size("loop"), lax.axis_size("hid")
    if n_loop == n_hid and slab % 128 == 0 and share % 128 == 0 and experts == n_hid:
        return tuple(compact(*args))
    return general(*args)


def solution(mesh):
    in_specs = (
        P(("groups", "loop"), None),
        P(("groups", "loop"), None),
        P(("groups", "loop"), None),
        P(("groups", "loop")),
        P(("groups", "loop")),
        P(None, None, "hid", "loop"),
    )
    out_specs = (P(("groups", "loop"), "hid"), P(("groups", "loop"), "hid"))
    return jax.shard_map(local, mesh=mesh, in_specs=in_specs, out_specs=out_specs, check_vma=False)
```

```python
import functools

import jax
import jax.numpy as jnp
from jax import lax
from jax.experimental import pallas as pl
from jax.experimental.pallas import tpu as pltpu
from jax.sharding import PartitionSpec as P

NODES = 64
CAP = 32
MESH = pl.DeviceIdType.MESH
SENT = jnp.bfloat16


def moe_kernel(
    n, ids_hbm, rw_hbm, acc_hbm, tok_hbm, w_hbm, sums_ref, place_ref,
    ids_ref, rw_ref, acc_ref, tok_ref, w,
    xsend, xbuf, pown, psend, pbuf, hbuf, fsend, rbuf, tsend, fin,
    in_sem, w_sem, xs_sem, xf_sem, xr_sem, ps_sem, pr_sem, hs_sem, hr_sem,
    rs_sem, rr_sem, ts_sem, tr_sem,
):
    me = lax.axis_index("loop")
    hid = lax.axis_index("hid")
    rows, width = tok_ref.shape
    experts, _, share, slab = w.shape
    slots = experts * CAP
    on_diag = me == hid
    others = list(range(1, n))

    def plus(index, k):
        return lax.rem(index + k, n)

    def minus(index, k):
        return lax.rem(index + n - k, n)

    barrier = pltpu.get_barrier_semaphore()
    for k in others:
        pl.semaphore_signal(barrier, inc=1, device_id={"loop": plus(me, k)}, device_id_type=MESH)
        pl.semaphore_signal(barrier, inc=1, device_id={"hid": plus(hid, k)}, device_id_type=MESH)

    @pl.when(jnp.logical_not(on_diag))
    def _():
        pl.semaphore_signal(barrier, inc=1, device_id={"loop": hid, "hid": me}, device_id_type=MESH)

    inputs = [
        pltpu.make_async_copy(source, target, in_sem.at[i])
        for i, (source, target) in enumerate(
            [(ids_hbm, ids_ref), (rw_hbm, rw_ref), (acc_hbm, acc_ref), (tok_hbm, tok_ref)]
        )
    ]
    for copy in inputs:
        copy.start()
    w_copies = [pltpu.make_async_copy(w_hbm.at[e], w.at[e], w_sem.at[e]) for e in range(experts)]
    for copy in w_copies:
        copy.start()

    f32, bf16 = jnp.float32, jnp.bfloat16
    r_i = lax.broadcasted_iota(jnp.int32, (rows, rows), 0)
    c_i = lax.broadcasted_iota(jnp.int32, (rows, rows), 1)
    upper = jnp.where(r_i < c_i, 1.0, 0.0).astype(bf16)
    slot = lax.broadcasted_iota(jnp.int32, (slots, rows), 0)
    slot_e = slot // CAP
    slot_i = (slot - slot_e * CAP).astype(f32)
    for copy in inputs:
        copy.wait()
    live = acc_ref[...] > 0
    ids = ids_ref[...]
    rw = rw_ref[...]
    match = jnp.zeros((slots, rows), f32)
    factor = jnp.zeros((slots, rows), f32)
    for e in range(experts):
        hit = (ids == e) & live
        m_e = jnp.sum(jnp.where(hit, 1.0, 0.0), axis=0, keepdims=True)
        f_e = jnp.sum(jnp.where(hit, rw, 0.0), axis=0, keepdims=True)
        match = jnp.where(slot_e == e, m_e, match)
        factor = jnp.where(slot_e == e, f_e, factor)
    rank = jnp.dot(match.astype(bf16), upper, preferred_element_type=f32)
    picked = (match > 0.0) & (rank == slot_i)
    place_t = jnp.where(picked, 1.0, 0.0)
    factor_col = jnp.sum(jnp.where(picked, factor, 0.0), axis=1, keepdims=True)
    place_t16 = place_t.astype(bf16)

    for k in others + [0]:
        cols = pl.ds(pl.multiple_of(plus(me, k) * slab, slab), slab)
        chosen = jnp.dot(place_t16, tok_ref[:, cols], preferred_element_type=f32)
        chosen = chosen.astype(bf16).reshape(experts, CAP, slab)
        if k == 0:
            xbuf[0] = chosen
        else:
            xsend[k - 1] = chosen

    @pl.when(on_diag)
    def _():
        pl.semaphore_wait(barrier, 2 * (n - 1))

    @pl.when(jnp.logical_not(on_diag))
    def _():
        pl.semaphore_wait(barrier, 2 * (n - 1) + 1)

    def x_copy(k, e):
        return pltpu.make_async_remote_copy(
            src_ref=xsend.at[k - 1, e], dst_ref=xbuf.at[k, e],
            send_sem=xs_sem.at[k - 1], recv_sem=xr_sem.at[k - 1, e],
            device_id={"loop": plus(me, k)}, device_id_type=MESH,
        )

    def x_forward(k, j):
        return pltpu.make_async_remote_copy(
            src_ref=xbuf.at[k, hid], dst_ref=xbuf.at[k, hid],
            send_sem=xf_sem.at[k - 1, j - 1], recv_sem=xr_sem.at[k - 1, hid],
            device_id={"hid": plus(hid, j)}, device_id_type=MESH,
        )

    def p_copy(k, e):
        return pltpu.make_async_remote_copy(
            src_ref=psend.at[e, k - 1], dst_ref=pbuf.at[k - 1, e],
            send_sem=ps_sem.at[k - 1, e], recv_sem=pr_sem.at[k - 1, e],
            device_id={"loop": minus(me, k)}, device_id_type=MESH,
        )

    def h_copy(k, e):
        return pltpu.make_async_remote_copy(
            src_ref=hbuf.at[e, 0], dst_ref=hbuf.at[e, k],
            send_sem=hs_sem.at[k - 1, e], recv_sem=hr_sem.at[k - 1, e],
            device_id={"loop": plus(me, k)}, device_id_type=MESH,
        )

    def r_copy(j, e):
        return pltpu.make_async_remote_copy(
            src_ref=fsend.at[e, minus(me, plus(hid, j))], dst_ref=rbuf.at[j - 1, e],
            send_sem=rs_sem.at[j - 1, e], recv_sem=rr_sem.at[j - 1, e],
            device_id={"hid": plus(hid, j)}, device_id_type=MESH,
        )

    def t_copy(e):
        return pltpu.make_async_remote_copy(
            src_ref=tsend.at[e], dst_ref=fin.at[e],
            send_sem=ts_sem.at[e], recv_sem=tr_sem.at[e],
            device_id={"loop": hid, "hid": me}, device_id_type=MESH,
        )

    for k in others:
        x_copy(k, hid).start()
    for k in others:
        x_copy(k, hid).wait_recv()
        for j in others:
            x_forward(k, j).start()

    def project(e):
        pltpu.make_async_copy(w_hbm.at[e], w.at[e], w_sem.at[e]).wait()
        part = lax.dot_general(
            xbuf[:, e].reshape(n * CAP, slab), w[e, 0:2].reshape(2 * share, slab),
            (((1,), (1,)), ((), ())), preferred_element_type=f32,
        )
        pown[e] = part[:CAP]
        psend[e] = part[CAP:].astype(SENT).reshape(n - 1, CAP, 2 * share)
        for k in others[1:] + others[:1]:
            p_copy(k, e).start()

    def project_other(e):
        @pl.when(hid != e)
        def _():
            for k in others:
                x_copy(k, e).wait_recv()
            project(e)

    def activate(e):
        for k in others:
            p_copy(k, e).wait_recv()
        total = pown[e]
        for k in others:
            total = total + pbuf[k - 1, e].astype(f32)
        gate, up = total[:, :share], total[:, share:]
        col = factor_col[e * CAP:(e + 1) * CAP]
        hbuf[e, 0] = (col * (gate / (1.0 + jnp.exp(-gate))) * up).astype(bf16)
        for k in others:
            h_copy(k, e).start()

    def down(e):
        for k in others:
            h_copy(k, e).wait_recv()
        fsend[e] = jnp.dot(
            hbuf[e].reshape(n * CAP, share), w[e, 2], preferred_element_type=f32
        ).reshape(n, CAP, slab)
        for j in others:
            r_copy(j, e).start()

    def collect(e):
        for j in others:
            r_copy(j, e).wait_recv()
        total = fsend[e, minus(me, hid)]
        for j in others:
            total = total + rbuf[j - 1, e]

        @pl.when(on_diag)
        def _():
            fin[e] = total.astype(bf16)

        @pl.when(jnp.logical_not(on_diag))
        def _():
            tsend[e] = total.astype(bf16)
            t_copy(e).start()

    project(hid)
    project_other(0)
    project_other(1)
    place_ref[...] = jnp.transpose(place_t).astype(bf16)
    for turn in range(experts + 2):
        if turn + 2 < experts:
            project_other(turn + 2)
        if turn < experts:
            activate(turn)
        if 0 <= turn - 1 < experts:
            down(turn - 1)
        if 0 <= turn - 2 < experts:
            collect(turn - 2)

    @pl.when(jnp.logical_not(on_diag))
    def _():
        for e in range(experts):
            t_copy(e).wait_recv()

    sums_ref[...] = fin[...].reshape(slots, slab)

    for k in others:
        x_copy(k, hid).wait_send()
        for j in others:
            x_forward(k, j).wait_send()
        for e in range(experts):
            p_copy(k, e).wait_send()
            h_copy(k, e).wait_send()
            r_copy(k, e).wait_send()

    @pl.when(jnp.logical_not(on_diag))
    def _():
        for e in range(experts):
            t_copy(e).wait_send()


def rows_kernel(sums_ref, place_ref, par_ref, out_ref, pout_ref):
    rows = place_ref.shape[0]
    f32, bf16 = jnp.float32, jnp.bfloat16
    r_i = lax.broadcasted_iota(jnp.int32, (rows, rows), 0)
    c_i = lax.broadcasted_iota(jnp.int32, (rows, rows), 1)
    family_t = jnp.where(r_i == c_i // NODES * NODES + par_ref[...], 1.0, 0.0)
    family = jnp.transpose(family_t).astype(bf16)
    value = jnp.dot(place_ref[...], sums_ref[...], preferred_element_type=f32).astype(bf16)
    out_ref[...] = value
    pout_ref[...] = jnp.dot(family, value, preferred_element_type=f32).astype(bf16)


def compact(tokens, route_ids, router_weights, accepted, parents, expert_weights):
    n = lax.axis_size("loop")
    rows = tokens.shape[0]
    experts, _, share, slab = expert_weights.shape
    bf16, f32 = jnp.bfloat16, jnp.float32
    vmem = pl.BlockSpec(memory_space=pltpu.VMEM)
    dma = pltpu.SemaphoreType.DMA
    args = (
        route_ids.T, router_weights.T, accepted.reshape(1, rows),
        tokens, expert_weights,
    )
    sums, place = pl.pallas_call(
        functools.partial(moe_kernel, n),
        out_shape=[
            jax.ShapeDtypeStruct((experts * CAP, slab), bf16),
            jax.ShapeDtypeStruct((rows, experts * CAP), bf16),
        ],
        in_specs=[pl.BlockSpec(memory_space=pltpu.HBM)] * 5,
        out_specs=[vmem] * 2,
        scratch_shapes=[pltpu.VMEM(a.shape, a.dtype) for a in args] + [
            pltpu.VMEM((n - 1, experts, CAP, slab), bf16),
            pltpu.VMEM((n, experts, CAP, slab), bf16),
            pltpu.VMEM((experts, CAP, 2 * share), f32),
            pltpu.VMEM((experts, n - 1, CAP, 2 * share), SENT),
            pltpu.VMEM((n - 1, experts, CAP, 2 * share), SENT),
            pltpu.VMEM((experts, n, CAP, share), bf16),
            pltpu.VMEM((experts, n, CAP, slab), f32),
            pltpu.VMEM((n - 1, experts, CAP, slab), f32),
            pltpu.VMEM((experts, CAP, slab), bf16),
            pltpu.VMEM((experts, CAP, slab), bf16),
            dma((4,)), dma((experts,)),
            dma((n - 1,)), dma((n - 1, n - 1)), dma((n - 1, experts)),
            dma((n - 1, experts)), dma((n - 1, experts)),
            dma((n - 1, experts)), dma((n - 1, experts)),
            dma((n - 1, experts)), dma((n - 1, experts)),
            dma((experts,)), dma((experts,)),
        ],
        compiler_params=pltpu.CompilerParams(
            collective_id=0, has_side_effects=True, vmem_limit_bytes=60 << 20
        ),
    )(*args)
    return pl.pallas_call(
        rows_kernel,
        out_shape=[jax.ShapeDtypeStruct((rows, slab), bf16)] * 2,
        in_specs=[vmem] * 3,
        out_specs=[vmem] * 2,
    )(sums, place, parents.reshape(1, rows))


def shifted(value, axis, by):
    devices = lax.axis_size(axis)
    return lax.ppermute(value, axis, [(i, (i + by) % devices) for i in range(devices)])


def move_one(piece, phase_name):
    if phase_name == "proj":
        return shifted(piece, "loop", 1)
    return shifted(piece, "loop", 1)


def rotate(piece, start_value, add_piece, phase_name):
    n_loop = lax.axis_size("loop")
    own_index = lax.axis_index("loop")
    total = add_piece(start_value, piece, own_index)

    def turn_body(turn_no, carried):
        arrived = move_one(carried[0], phase_name)
        anchor = jnp.mod(own_index - turn_no, n_loop)
        return (arrived, add_piece(carried[1], arrived, anchor))

    carried = lax.fori_loop(1, n_loop, turn_body, (piece, total))
    return carried[1]


def general(tokens, route_ids, router_weights, accepted, parents, expert_weights):
    row_count = tokens.shape[0]
    model_width = tokens.shape[1]
    window_count = expert_weights.shape[0]
    hidden_share = expert_weights.shape[2]
    slab_width = expert_weights.shape[3]
    proj_weights = expert_weights[:, 0:2]
    down_weights = expert_weights[:, 2]
    matches = route_ids[:, :, None] == jnp.arange(window_count, dtype=jnp.int32)[None, None, :]
    live_rows = accepted > 0
    combine = jnp.where(
        live_rows[:, None],
        jnp.sum(jnp.where(matches, router_weights[:, :, None], 0.0), axis=1),
        0.0,
    )

    def proj_piece(total, piece, anchor):
        columns = lax.dynamic_slice_in_dim(tokens, anchor * slab_width, slab_width, 1)
        return total + jnp.einsum(
            "rd,etfd->retf", columns, piece, preferred_element_type=jnp.float32
        )

    proj_start = jnp.zeros((row_count, window_count, 2, hidden_share), jnp.float32)
    projected = rotate(proj_weights, proj_start, proj_piece, "proj")
    weighted = (combine[:, :, None] * jax.nn.silu(projected[:, :, 0]) * projected[:, :, 1]).astype(
        jnp.bfloat16
    )

    def down_piece(total, piece, anchor):
        block = jnp.einsum("ref,efd->rd", weighted, piece, preferred_element_type=jnp.float32)
        return lax.dynamic_update_slice_in_dim(total, block, anchor * slab_width, 1)

    partial_value = rotate(
        down_weights, jnp.zeros((row_count, model_width), jnp.float32), down_piece, "down"
    )
    share_width = model_width // lax.axis_size("hid")
    summed_all = lax.psum(partial_value, "hid")
    expert_out = lax.dynamic_slice_in_dim(
        summed_all, lax.axis_index("hid") * share_width, share_width, 1
    ).astype(jnp.bfloat16)
    tree_count = row_count // NODES
    family = jax.nn.one_hot(parents.reshape(tree_count, NODES), NODES, dtype=jnp.bfloat16)
    grouped = expert_out.reshape(tree_count, NODES, share_width)
    parent_out = jnp.einsum("qnm,qmd->qnd", family, grouped, preferred_element_type=jnp.float32)
    parent_out = parent_out.astype(jnp.bfloat16).reshape(row_count, share_width)
    return (expert_out, parent_out)


def local(tokens, route_ids, router_weights, accepted, parents, expert_weights):
    args = (tokens, route_ids, router_weights, accepted, parents, expert_weights)
    experts, _, share, slab = expert_weights.shape
    n_loop, n_hid = lax.axis_size("loop"), lax.axis_size("hid")
    if n_loop == n_hid and slab % 128 == 0 and share % 128 == 0 and experts == n_hid:
        return tuple(compact(*args))
    return general(*args)


def solution(mesh):
    in_specs = (
        P(("groups", "loop"), None),
        P(("groups", "loop"), None),
        P(("groups", "loop"), None),
        P(("groups", "loop")),
        P(("groups", "loop")),
        P(None, None, "hid", "loop"),
    )
    out_specs = (P(("groups", "loop"), "hid"), P(("groups", "loop"), "hid"))
    return jax.shard_map(local, mesh=mesh, in_specs=in_specs, out_specs=out_specs, check_vma=False)
```
